256 devices in a mesh: ep: 64 (over z_lo, y, x), dp: 4 (over z_hi, core).
Axes of the slice: x: 4, y: 4, z: 8 (z_hi: 2, z_lo: 4; z = z_hi * 4 + z_lo), core: 2. Of those that a mesh axis runs over, the one named last changes fastest.
Arguments:
- tokens: bfloat16 [32768, 1792], P(('ep', 'dp')), may hold values from -6 to 6
- cotangent: bfloat16 [32768, 1792], P(('ep', 'dp')), may hold values from -6 to 6
- slot_choice: int32 [32768, 2], P(('ep', 'dp')), may hold values from 0 to 63, all different within a row; in each aligned block of 128 rows (0 to 127, 128 to 255, ...) at most 5 rows name the same one
- gate_values: float32 [32768, 2], P(('ep', 'dp')), may hold values from 0.1 to 1
- slot_expert: int32 [64], replicated, may hold values from 0 to 31, as said below
- gate_weight: bfloat16 [64, 1792, 1280], P('ep', None, 'dp'), as said below
- up_weight: bfloat16 [64, 1792, 1280], P('ep', None, 'dp'), as said below
- down_weight: bfloat16 [64, 1280, 1792], P('ep', 'dp'), as said below
Outputs:
- token_grad: bfloat16 [32768, 1792], P(('ep', 'dp'))
- down_grad: bfloat16 [64, 1280, 1792], P('ep', 'dp')
The draws below stay inside these ranges and needn't reach their ends.
Inputs may be any that keep to these rules, and one draw needn't show every extreme that they name: `slot_choice`: each row names 2 different slots; among the rows of one device no slot is named more than 5 times, a bound that some block reaches. `slot_expert`: every expert is held by at least one slot. `gate_weight`: slots that hold the same expert have equal matrices. `up_weight`: slots that hold the same expert have equal matrices. `down_weight`: slots that hold the same expert have equal matrices.
All inputs are finite; a program needn't handle non-finite values.
Results may differ from the reference program's by a relative error of at most 0.0098.
Values may be sent and summed in bfloat16 or wider, within the bound.
No kernel may reach another device: no remote copies, remote signals or barrier semaphores. Data moves between devices by JAX's collectives and lax.ppermute only.
A program may use at most 128 MiB of HBM per device.

```python
import math
import jax
import jax.numpy as jnp
import numpy as np
from jax import lax

D = 1792
FF = 1280
TOPK = 2
TOK_DEV = 128
SLOTS = 64
EXPERTS = 32
CAP = 5
TOKENS = 32768


def holder_table(key):
    primary = jnp.arange(EXPERTS, dtype=jnp.int32)
    extra = jax.random.randint(jax.random.fold_in(key, 101), (SLOTS - EXPERTS,), 0, EXPERTS, dtype=jnp.int32)
    order = jax.random.permutation(jax.random.fold_in(key, 102), SLOTS)
    return jnp.concatenate([primary, extra])[order]


def expert_matrices(key, salt, shape, fan):
    base = jax.random.normal(jax.random.fold_in(key, salt), shape, jnp.float32) * fan ** (-0.5)
    return base[holder_table(key)].astype(jnp.bfloat16)


def draw_slot_expert(key, part):
    return holder_table(key)


def draw_gate_weight(key, part):
    return expert_matrices(key, 201, (EXPERTS, D, FF), D)


def draw_up_weight(key, part):
    return expert_matrices(key, 202, (EXPERTS, D, FF), D)


def draw_down_weight(key, part):
    return expert_matrices(key, 203, (EXPERTS, FF, D), FF)


def levels(rng, extent, cuts, smallest, largest):
    level = 1.0
    for dim, parts in cuts:
        heights = jax.random.uniform(jax.random.fold_in(jax.random.fold_in(rng, 6), dim), (parts,), jnp.float32, smallest / len(cuts), largest / len(cuts))
        level = level * jnp.repeat(jnp.exp(heights), extent[dim] // parts).reshape((-1,) + (1,) * (len(extent) - 1 - dim))
    return level


def shared_out(stream_key, own, number, rows, number_of, top, limit, lean):
    order = jax.random.permutation(stream_key, number_of)
    heavy_load, usual = shares(number_of, rows * top, limit, lean, True), shares(number_of, rows * top, limit, lean, False)
    places = jnp.arange(number_of)

    def named(lengths, rotation):
        used = int((lengths > 0).sum())
        fixed = max(1, used // 4)
        moved = fixed + (places - fixed + rotation * (used - fixed)) % max(1, number_of - fixed)
        return jnp.zeros((number_of,), jnp.int32).at[order[jnp.where(places < fixed, places, moved)]].set(jnp.asarray(lengths, jnp.int32))

    lengths = jnp.where(number % 4 == 0, named(heavy_load, number // 4), named(usual, number - number // 4 - 1))
    mixed = jax.random.permutation(jax.random.fold_in(own, 3), number_of)
    source_of, receiver = mixed[0:number_of // 2 * 2:2], mixed[1:number_of // 2 * 2:2]
    margin = jnp.minimum(lengths[source_of] - 1, limit - lengths[receiver]) // 2
    margin = jnp.where((source_of == order[0]) | (receiver == order[0]) | (lengths[receiver] == 0), 0, jnp.maximum(margin, 0))
    moved = jax.random.randint(jax.random.fold_in(own, 4), (number_of // 2,), 0, 1 << 20) % (margin + 1)
    lengths = lengths.at[source_of].add(-moved).at[receiver].add(moved)
    items = jnp.searchsorted(jnp.cumsum(lengths), jnp.arange(rows * top), side="right").astype(jnp.int32)
    grid = items.reshape(top, rows).T
    grid = grid[jax.random.permutation(jax.random.fold_in(own, 1), rows)]
    rotation = jax.random.randint(jax.random.fold_in(own, 2), (rows, 1), 0, top)
    return jnp.take_along_axis(grid, (jnp.arange(top)[None, :] + rotation) % top, axis=1)


def shares(count, total, most, skew, full):
    portions = [(1 << 20) // math.isqrt(grade ** skew) + 1 for grade in range(1, count + 1)]
    largest = most if full else min(most, max(-(-total // count), total * portions[0] // sum(portions)))
    least = 1 if total - largest >= count - 1 else 0
    holding, rest = [largest] + [least] * (count - 1), total - largest - least * (count - 1)
    while rest > 0:
        free = [i for i in range(1, count) if holding[i] < largest] or [i for i in range(1, count) if holding[i] < most]
        pool, budget = sum([portions[i] for i in free]), rest
        for i in free:
            more = min(most - holding[i], max(1, budget * portions[i] // pool), rest)
            holding[i] = holding[i] + more
            rest = rest - more
    return np.array(holding)


def gaussian(stream_key, extent, spread, most, shards=(), held_as=jnp.bfloat16):
    level = levels(stream_key, extent, shards, -0.22, 0.18) if shards else 1.0
    entries = jax.random.normal(stream_key, extent, jnp.float32) * spread * level
    return jnp.minimum(jnp.maximum(entries, -most), most).astype(held_as)


def setup_inputs(seed: int = 0) -> dict:
    streams_of = jax.random.split(jax.random.key(seed), 9)
    tokens = gaussian(streams_of[0], (TOKENS, D), 1.0, 6.0, ((0, 256),))
    cotangent = gaussian(streams_of[1], (TOKENS, D), 1.0, 6.0, ((0, 256),))
    slot_choice_keys = jax.random.split(jax.random.fold_in(streams_of[2], 1), TOKENS // TOK_DEV)
    slot_choice_turns = jax.random.permutation(jax.random.fold_in(streams_of[2], 3), TOKENS // TOK_DEV)
    slot_choice = jax.vmap(lambda own, number: shared_out(jax.random.fold_in(streams_of[2], 2), own, number, TOK_DEV, SLOTS, TOPK, CAP, 2))(slot_choice_keys, slot_choice_turns).reshape((TOKENS, TOPK))
    gate_values = jnp.clip(jnp.exp(math.log(1.0) - 2.3025851 * jax.random.uniform(streams_of[3], (TOKENS, TOPK), jnp.float32) ** levels(streams_of[3], (TOKENS, TOPK), ((0, 256),), -0.2, 0.2)), 0.1, 1.0)
    slot_expert = draw_slot_expert(jax.random.fold_in(streams_of[8], 71), 0)
    gate_weight = draw_gate_weight(jax.random.fold_in(streams_of[8], 71), 0)
    up_weight = draw_up_weight(jax.random.fold_in(streams_of[8], 71), 0)
    down_weight = draw_down_weight(jax.random.fold_in(streams_of[8], 71), 0)
    return dict(tokens=tokens, cotangent=cotangent, slot_choice=slot_choice, gate_values=gate_values, slot_expert=slot_expert, gate_weight=gate_weight, up_weight=up_weight, down_weight=down_weight)


def slot_backward(operands):
    rows_x, rows_g, w_gate, w_up, w_down = operands
    gate = jnp.dot(rows_x, w_gate, preferred_element_type=jnp.float32)
    up = jnp.dot(rows_x, w_up, preferred_element_type=jnp.float32)
    sig = jax.nn.sigmoid(gate)
    act = (gate * sig * up).astype(jnp.bfloat16)
    d_act = jnp.dot(rows_g, w_down.T, preferred_element_type=jnp.float32)
    d_gate = (d_act * up * sig * (1.0 + gate * (1.0 - sig))).astype(jnp.bfloat16)
    d_up = (d_act * gate * sig).astype(jnp.bfloat16)
    contrib = jnp.dot(d_gate, w_gate.T, preferred_element_type=jnp.float32)
    contrib = contrib + jnp.dot(d_up, w_up.T, preferred_element_type=jnp.float32)
    grad = jnp.dot(act.T, rows_g, preferred_element_type=jnp.float32)
    return contrib.astype(jnp.bfloat16), grad


def reference(tokens, cotangent, slot_choice, gate_values, slot_expert, gate_weight, up_weight, down_weight):
    blocks = TOKENS // TOK_DEV
    items = TOK_DEV * TOPK
    choice_b = slot_choice.reshape(blocks, items).astype(jnp.int32)
    onehot = (choice_b[:, :, None] == jnp.arange(SLOTS, dtype=jnp.int32)[None, None, :]).astype(jnp.int32)
    position = jnp.sum(jnp.cumsum(onehot, axis=1) * onehot, axis=2) - 1
    block_id = jnp.arange(blocks, dtype=jnp.int32)[:, None]
    dest = (choice_b * (blocks * CAP) + block_id * CAP + position).reshape(-1).astype(jnp.int32)
    total_rows = SLOTS * blocks * CAP
    source = jnp.full((total_rows,), TOKENS * TOPK, jnp.int32)
    source = source.at[dest].set(jnp.arange(TOKENS * TOPK, dtype=jnp.int32))
    zero_row = jnp.zeros((1, D), jnp.bfloat16)
    item_x = jnp.concatenate([jnp.repeat(tokens, TOPK, axis=0), zero_row], axis=0)
    scaled = cotangent.astype(jnp.float32)[:, None, :] * gate_values.astype(jnp.float32)[:, :, None]
    scaled = scaled.reshape(TOKENS * TOPK, D).astype(jnp.bfloat16)
    item_g = jnp.concatenate([scaled, zero_row], axis=0)
    rows_x = item_x[source].reshape(SLOTS, blocks * CAP, D)
    rows_g = item_g[source].reshape(SLOTS, blocks * CAP, D)
    contrib, grads = lax.map(slot_backward, (rows_x, rows_g, gate_weight, up_weight, down_weight))
    picked = contrib.reshape(total_rows, D)[dest].astype(jnp.float32).reshape(TOKENS, TOPK, D)
    token_grad = jnp.sum(picked, axis=1).astype(jnp.bfloat16)
    same = (slot_expert[:, None] == slot_expert[None, :]).astype(jnp.float32)
    summed = jnp.einsum("st,tfd->sfd", same, grads, precision=lax.Precision.HIGHEST)
    return token_grad, summed.astype(jnp.bfloat16)
```

```python
import jax
import jax.numpy as jnp
from jax import lax
from jax.experimental import pallas as pl
from jax.experimental.pallas import tpu as pltpu
from jax.sharding import Mesh, PartitionSpec as P

CAP = 5
NZ = 8
PLANE = 16
EXPERTS = 32
INFO = 8
F32 = jnp.float32
BF16 = jnp.bfloat16


def dot(a, b, ca, cb):
    return lax.dot_general(a, b, (((ca,), (cb,)), ((), ())), preferred_element_type=F32)


def expert_sum_kernel(expert_ref, parts_ref, out_ref, total):
    total[...] = jnp.zeros_like(total)

    def add(r, carry):
        e = expert_ref[r]
        total[e] += parts_ref[r].astype(F32)
        return carry

    def put(s, carry):
        out_ref[s] = total[expert_ref[s]].astype(BF16)
        return carry

    lax.fori_loop(0, parts_ref.shape[0], add, 0)
    lax.fori_loop(0, parts_ref.shape[0], put, 0)


def expert_sum(slot_expert, parts):
    return pl.pallas_call(
        expert_sum_kernel,
        out_shape=jax.ShapeDtypeStruct(parts.shape, BF16),
        in_specs=[
            pl.BlockSpec(memory_space=pltpu.SMEM),
            pl.BlockSpec(memory_space=pltpu.VMEM),
        ],
        out_specs=pl.BlockSpec(memory_space=pltpu.VMEM),
        scratch_shapes=[pltpu.VMEM((EXPERTS, *parts.shape[1:]), F32)],
        compiler_params=pltpu.CompilerParams(vmem_limit_bytes=16 * 2**20),
    )(slot_expert, parts)


def per_device(
    tokens, cotangent, slot_choice, gate_values, slot_expert, gate_weight, up_weight, down_weight
):
    rows, width = tokens.shape
    items = 2 * rows
    z_lo = lax.axis_index("zl")
    slot = slot_choice.T.reshape(items)
    weight = gate_values.T.reshape(items)
    order = jnp.arange(items, dtype=jnp.int32)
    earlier = (slot[:, None] == slot[None, :]) & (order[None, :] < order[:, None])
    place = jnp.sum(earlier.astype(jnp.int32), axis=1)
    high = lax.reduce_precision(weight, 8, 7)
    middle = lax.reduce_precision(weight - high, 8, 7)
    low = weight - high - middle
    facts = jnp.stack([slot.astype(F32), place.astype(F32), high, middle, low]).astype(BF16)
    facts = jnp.pad(facts, ((0, INFO - facts.shape[0]), (0, width - items)))
    sent = jnp.concatenate([tokens, facts], axis=0)
    block = rows + INFO

    all_x = lax.all_gather(sent, ("zh", "zl"), axis=0, tiled=True)
    all_g = lax.all_gather(cotangent, ("zh", "zl"), axis=0, tiled=True)

    info = all_x.reshape(NZ, block, width)[:, rows : rows + 5, :items].astype(F32)
    info = info.reshape(NZ, 5, 2, rows)
    source = jnp.arange(NZ, dtype=jnp.int32)[:, None, None]
    code = info[:, 0].astype(jnp.int32) - z_lo * PLANE
    here = (code >= 0) & (code < PLANE)
    code = jnp.where(here, (code * NZ + source) * CAP + info[:, 1].astype(jnp.int32), -1)
    strength = info[:, 2] + info[:, 3] + info[:, 4]
    code = jnp.moveaxis(code, 1, 0)
    strength = jnp.moveaxis(strength, 1, 0)
    held = PLANE * NZ * CAP
    row_ids = jnp.arange(held, dtype=jnp.int32)[:, None]

    code_pad = jnp.pad(code, ((0, 0), (0, 0), (0, INFO)), constant_values=-1).reshape(2, NZ * block)
    pick_x = ((code_pad[0][None, :] == row_ids) | (code_pad[1][None, :] == row_ids)).astype(BF16)
    code = code.reshape(2, NZ * rows)
    strength = strength.reshape(2, NZ * rows)
    first, second = code[0][None, :] == row_ids, code[1][None, :] == row_ids
    pick = (first | second).astype(BF16)
    scale = jnp.sum(
        jnp.where(first, strength[0][None, :], 0.0) + jnp.where(second, strength[1][None, :], 0.0),
        axis=1,
        keepdims=True,
    )
    sent_x = dot(pick_x, all_x, 1, 0).astype(BF16)
    own_x = lax.all_to_all(
        sent_x.reshape(PLANE, NZ * CAP, width), ("y", "x"), split_axis=0, concat_axis=0, tiled=True
    ).reshape(held, width)
    swap = [(0, 1), (1, 0)]
    other_x = lax.ppermute(own_x, "c", swap)
    sent_g = (dot(pick, all_g, 1, 0) * scale).astype(BF16)
    own_g = lax.all_to_all(
        sent_g.reshape(PLANE, NZ * CAP, width), ("y", "x"), split_axis=0, concat_axis=0, tiled=True
    ).reshape(held, width)
    other_g = lax.ppermute(own_g, "c", swap)

    w_gate, w_up, w_down = gate_weight[0], up_weight[0], down_weight[0]

    def half(x, g):
        gate, up = dot(x, w_gate, 1, 0), dot(x, w_up, 1, 0)
        sig = jax.nn.sigmoid(gate)
        act = (gate * sig * up).astype(BF16)
        d_act = dot(g, w_down, 1, 1)
        d_gate = (d_act * up * sig * (1.0 + gate * (1.0 - sig))).astype(BF16)
        d_up = (d_act * gate * sig).astype(BF16)
        return act, d_gate, d_up

    act_o, d_gate_o, d_up_o = half(other_x, other_g)
    for_other = (dot(d_gate_o, w_gate, 1, 1) + dot(d_up_o, w_up, 1, 1)).astype(BF16)
    from_other = lax.ppermute(for_other, "c", swap)
    act, d_gate, d_up = half(own_x, own_g)
    slot_grad = dot(act, own_g, 0, 0) + dot(act_o, other_g, 0, 0)
    own = dot(d_gate, w_gate, 1, 1) + dot(d_up, w_up, 1, 1)
    contribution = (own + from_other.astype(F32)).astype(BF16)

    back = lax.all_to_all(
        contribution.reshape(PLANE, NZ * CAP, width),
        ("y", "x"),
        split_axis=0,
        concat_axis=0,
        tiled=True,
    ).reshape(held, width)
    partial = dot(pick, back, 0, 0).astype(BF16)
    token_grad = lax.psum_scatter(partial, ("zh", "zl"), scatter_dimension=0, tiled=True)

    hidden = slot_grad.shape[0]
    down, across = hidden // 8, width // 128
    n_slots = slot_expert.shape[0]
    each = -(-down * across // n_slots)
    tiles = slot_grad.astype(BF16).reshape(down, 8, across, 128).transpose(0, 2, 1, 3)
    tiles = tiles.reshape(down * across, 8, 128)
    tiles = jnp.pad(tiles, ((0, each * n_slots - down * across), (0, 0), (0, 0)))
    tiles = tiles.reshape(n_slots, each * 8, 128)
    axes = ("zl", "y", "x")
    parts = lax.all_to_all(tiles, axes, split_axis=0, concat_axis=0, tiled=True)
    summed = expert_sum(slot_expert, parts)
    summed = lax.all_to_all(summed, axes, split_axis=0, concat_axis=0, tiled=True)
    summed = summed.reshape(n_slots * each, 8, 128)[: down * across]
    down_grad = summed.reshape(down, across, 8, 128).transpose(0, 2, 1, 3).reshape(1, hidden, width)
    return token_grad, down_grad


def solution(mesh):
    fine = Mesh(mesh.devices.reshape(4, 4, 4, 2, 2), ("zl", "y", "x", "zh", "c"))
    ep, dp = ("zl", "y", "x"), ("zh", "c")
    token = P((*ep, *dp), None)
    return jax.shard_map(
        per_device,
        mesh=fine,
        in_specs=(token, token, token, token, P(), P(ep, None, dp), P(ep, None, dp), P(ep, dp, None)),
        out_specs=(token, P(ep, dp, None)),
        check_vma=False,
    )
```

```python
import jax
import jax.numpy as jnp
from jax import lax
from jax.experimental import pallas as pl
from jax.experimental.pallas import tpu as pltpu
from jax.sharding import Mesh, PartitionSpec as P

CAP = 5
NZ = 8
PLANE = 16
EXPERTS = 32
F32 = jnp.float32
BF16 = jnp.bfloat16


def dot(a, b, ca, cb):
    return lax.dot_general(a, b, (((ca,), (cb,)), ((), ())), preferred_element_type=F32)


def expert_sum_kernel(expert_ref, parts_ref, out_ref, total):
    count, planes = parts_ref.shape[:2]
    total[...] = jnp.zeros_like(total)

    def add(j, carry):
        for d in range(planes):
            total[expert_ref[d, j]] += parts_ref[j, d].astype(F32)
        return carry

    def put(j, carry):
        for d in range(planes):
            out_ref[j, d] = total[expert_ref[d, j]].astype(BF16)
        return carry

    lax.fori_loop(0, count, add, 0)
    lax.fori_loop(0, count, put, 0)


def expert_sum(expert, parts):
    whole = pl.BlockSpec(memory_space=pltpu.VMEM)
    return pl.pallas_call(
        expert_sum_kernel,
        out_shape=jax.ShapeDtypeStruct(parts.shape, BF16),
        in_specs=[pl.BlockSpec(memory_space=pltpu.SMEM), whole],
        out_specs=whole,
        scratch_shapes=[pltpu.VMEM((EXPERTS, *parts.shape[2:]), F32)],
        compiler_params=pltpu.CompilerParams(vmem_limit_bytes=12 * 2**20),
    )(expert, parts)


def exchange(rows):
    chunks = rows.reshape(PLANE, rows.shape[0] // PLANE, *rows.shape[1:])
    got = lax.all_to_all(chunks, ("y", "x"), split_axis=0, concat_axis=0, tiled=True)
    return got.reshape(rows.shape)


def swapped(rows):
    return lax.ppermute(rows, "c", [(0, 1), (1, 0)])


def after(value, *earlier):
    return lax.optimization_barrier((value, *earlier))[0]


def per_device(
    tokens, cotangent, slot_choice, gate_values, slot_expert, gate_weight, up_weight, down_weight
):
    rows, width = tokens.shape
    items = 2 * rows
    z_lo = lax.axis_index("zl")
    ring = ("zh", "zl")
    all_x = lax.all_gather(tokens, ring, axis=0, tiled=True)
    all_g = lax.all_gather(cotangent, ring, axis=0, tiled=True)

    slot = slot_choice.T.reshape(items)
    order = jnp.arange(items, dtype=jnp.int32)
    earlier = (slot[:, None] == slot[None, :]) & (order[None, :] < order[:, None])
    spot = slot * 8 + jnp.sum(earlier.astype(jnp.int32), axis=1)
    facts = jnp.concatenate([spot.astype(F32).reshape(2, rows), gate_values.T], axis=0)
    info = lax.all_gather(facts, ring, axis=0)
    spot, strength = info[:, :2].astype(jnp.int32), info[:, 2:]
    source = jnp.arange(NZ, dtype=jnp.int32)[:, None, None]
    code = spot // 8 - z_lo * PLANE
    here = (code >= 0) & (code < PLANE)
    code = jnp.where(here, (code * NZ + source) * CAP + spot % 8, -1)
    held = PLANE * NZ * CAP
    code = jnp.moveaxis(code, 1, 0).reshape(2, NZ * rows)
    strength = jnp.moveaxis(strength, 1, 0).reshape(2, NZ * rows)

    row_ids = jnp.arange(held, dtype=jnp.int32)[:, None]
    first, second = code[0][None, :] == row_ids, code[1][None, :] == row_ids
    scale = jnp.sum(
        jnp.where(first, strength[0][None, :], 0.0) + jnp.where(second, strength[1][None, :], 0.0),
        axis=1,
        keepdims=True,
    )
    pick, scale = lax.optimization_barrier(((first | second).astype(BF16), scale))

    w_gate, w_up, w_down = gate_weight[0], up_weight[0], down_weight[0]

    def forward(x):
        gate, up = dot(x, w_gate, 1, 0), dot(x, w_up, 1, 0)
        sig = jax.nn.sigmoid(gate)
        return (gate * sig * up).astype(BF16), up * sig * (1.0 + gate * (1.0 - sig)), gate * sig

    def backward(g, for_gate, for_up):
        d_act = dot(g, w_down, 1, 1)
        return (d_act * for_gate).astype(BF16), (d_act * for_up).astype(BF16)

    x = exchange(dot(pick, all_x, 1, 0).astype(BF16))
    x_o = swapped(x)
    sent_g = (dot(pick, after(all_g, x_o), 1, 0) * scale).astype(BF16)
    x, x_o, sent_g = lax.optimization_barrier((x, x_o, sent_g))
    g = exchange(sent_g)
    forwards = forward(x), forward(x_o)
    forwards, g = lax.optimization_barrier((forwards, g))
    (act, for_gate, for_up), (act_o, for_gate_o, for_up_o) = forwards
    g_o = swapped(g)
    slot_grad = dot(act, g, 0, 0) + dot(act_o, g_o, 0, 0)

    hidden = slot_grad.shape[0]
    down, across = hidden // 8, width // 128
    n_slots = slot_expert.shape[0]
    planes = n_slots // PLANE
    each = -(-down * across // n_slots)
    tiles = slot_grad.astype(BF16).reshape(down, 8, across, 128).transpose(0, 2, 1, 3)
    tiles = tiles.reshape(down * across, 8, 128)
    tiles = jnp.pad(tiles, ((0, each * n_slots - down * across), (0, 0), (0, 0)))
    tiles = tiles.reshape(planes, PLANE, each * 8, 128)

    def of_plane(v, d, dim):
        return lax.dynamic_index_in_dim(v, z_lo ^ d, dim, False)

    def along_z(piece, d):
        return lax.ppermute(piece, "zl", [(z, z ^ d) for z in range(planes)]) if d else piece

    sent = lax.optimization_barrier((g, g_o, *[of_plane(tiles, d, 0) for d in range(planes)]))
    g, g_o = sent[:2]
    pieces = [along_z(piece, d) for d, piece in enumerate(sent[2:])]

    d_gate_o, d_up_o = backward(g_o, for_gate_o, for_up_o)
    for_other = (dot(d_gate_o, w_gate, 1, 1) + dot(d_up_o, w_up, 1, 1)).astype(BF16)
    from_other = swapped(for_other)
    d_gate, d_up = backward(g, for_gate, for_up)
    own = dot(d_gate, w_gate, 1, 1) + dot(d_up, w_up, 1, 1)
    back = exchange((own + from_other.astype(F32)).astype(BF16))
    parts = jnp.stack(pieces, axis=1)
    back, parts = lax.optimization_barrier((back, parts))
    parts = exchange(parts)
    partial = dot(pick, back, 0, 0).astype(BF16)
    token_grad = lax.psum_scatter(partial, ring, scatter_dimension=0, tiled=True)

    expert = slot_expert.reshape(planes, PLANE)
    expert = jnp.stack([of_plane(expert, d, 0) for d in range(planes)])
    sums = exchange(expert_sum(expert, parts))
    summed = jnp.stack([along_z(sums[:, d], d) for d in range(planes)])
    summed = jnp.concatenate([of_plane(summed, z, 0) for z in range(planes)])
    summed = summed.reshape(n_slots * each, 8, 128)[: down * across]
    down_grad = summed.reshape(down, across, 8, 128).transpose(0, 2, 1, 3).reshape(1, hidden, width)
    return token_grad, down_grad


def solution(mesh):
    fine = Mesh(mesh.devices.reshape(4, 4, 4, 2, 2), ("zl", "y", "x", "zh", "c"))
    ep, dp = ("zl", "y", "x"), ("zh", "c")
    token = P((*ep, *dp), None)
    return jax.shard_map(
        per_device,
        mesh=fine,
        in_specs=(token, token, token, token, P(), P(ep, None, dp), P(ep, None, dp), P(ep, dp, None)),
        out_specs=(token, P(ep, dp, None)),
        check_vma=False,
    )
```

```python
import jax
import jax.numpy as jnp
from jax import lax
from jax.experimental import pallas as pl
from jax.experimental.pallas import tpu as pltpu
from jax.sharding import Mesh, PartitionSpec as P

CAP = 5
INFO = 8
NZ = 8
PLANE = 16
EXPERTS = 32
F32 = jnp.float32
BF16 = jnp.bfloat16


def dot(a, b, ca, cb):
    return lax.dot_general(a, b, (((ca,), (cb,)), ((), ())), preferred_element_type=F32)


def expert_sum_kernel(expert_ref, parts_ref, out_ref, total):
    count, planes = parts_ref.shape[:2]
    total[...] = jnp.zeros_like(total)

    def add(j, carry):
        for d in range(planes):
            total[expert_ref[d, j]] += parts_ref[j, d].astype(F32)
        return carry

    def put(j, carry):
        for d in range(planes):
            out_ref[j, d] = total[expert_ref[d, j]].astype(BF16)
        return carry

    lax.fori_loop(0, count, add, 0)
    lax.fori_loop(0, count, put, 0)


def expert_sum(expert, parts):
    whole = pl.BlockSpec(memory_space=pltpu.VMEM)
    return pl.pallas_call(
        expert_sum_kernel,
        out_shape=jax.ShapeDtypeStruct(parts.shape, BF16),
        in_specs=[pl.BlockSpec(memory_space=pltpu.SMEM), whole],
        out_specs=whole,
        scratch_shapes=[pltpu.VMEM((EXPERTS, *parts.shape[2:]), F32)],
        compiler_params=pltpu.CompilerParams(vmem_limit_bytes=12 * 2**20),
    )(expert, parts)


def exchange(rows):
    chunks = rows.reshape(PLANE, rows.shape[0] // PLANE, *rows.shape[1:])
    got = lax.all_to_all(chunks, ("y", "x"), split_axis=0, concat_axis=0, tiled=True)
    return got.reshape(rows.shape)


def swapped(rows):
    return lax.ppermute(rows, "c", [(0, 1), (1, 0)])


def after(value, *earlier):
    return lax.optimization_barrier((value, *earlier))[0]


def ring_steps(own):
    def at(z):
        return (z % NZ) % 4 * 2 + (z % NZ) // 4

    up = [(at(z), at(z + 1)) for z in range(NZ)]
    down = [(at(z), at(z - 1)) for z in range(NZ)]
    below, above = [own], [own]
    for step in range(NZ // 2):
        below.append(lax.ppermute(below[-1], ("zl", "zh"), up))
        if step < NZ // 2 - 1:
            above.append(lax.ppermute(above[-1], ("zl", "zh"), down))
    return above + below[:0:-1], (below[3], above[3])


def per_device(
    tokens, cotangent, slot_choice, gate_values, slot_expert, gate_weight, up_weight, down_weight
):
    rows, width = tokens.shape
    items = 2 * rows
    z_lo, z_hi = lax.axis_index("zl"), lax.axis_index("zh")
    turn = z_hi * 4 + z_lo
    ring = ("zh", "zl")
    slot = slot_choice.T.reshape(items)
    weight = gate_values.T.reshape(items)
    order = jnp.arange(items, dtype=jnp.int32)
    earlier = (slot[:, None] == slot[None, :]) & (order[None, :] < order[:, None])
    place = jnp.sum(earlier.astype(jnp.int32), axis=1)
    high = lax.reduce_precision(weight, 8, 7)
    middle = lax.reduce_precision(weight - high, 8, 7)
    low = weight - high - middle
    facts = jnp.stack([slot.astype(F32), place.astype(F32), high, middle, low]).astype(BF16)
    facts = jnp.pad(facts, ((0, INFO - facts.shape[0]), (0, width - items)))
    block = rows + INFO

    x_pieces, started = ring_steps(jnp.concatenate([tokens, facts], axis=0))
    all_g = lax.all_gather(after(cotangent, *started), ring, axis=0, tiled=True)

    info = jnp.stack([p[rows : rows + 5, :items] for p in x_pieces]).astype(F32).reshape(NZ, 5, 2, rows)
    source = ((jnp.arange(NZ, dtype=jnp.int32) + turn) % NZ)[:, None, None]
    code = info[:, 0].astype(jnp.int32) - z_lo * PLANE
    here = (code >= 0) & (code < PLANE)
    code = jnp.where(here, (code * NZ + source) * CAP + info[:, 1].astype(jnp.int32), -1)
    strength = info[:, 2] + info[:, 3] + info[:, 4]
    held = PLANE * NZ * CAP
    row_ids = jnp.arange(held, dtype=jnp.int32)[:, None]

    def flat(v):
        return jnp.moveaxis(v, 1, 0).reshape(2, -1)

    def from_zero(v):
        return flat(lax.dynamic_slice_in_dim(jnp.concatenate([v, v], axis=0), NZ - turn, NZ, axis=0))

    code_x = flat(jnp.pad(code, ((0, 0), (0, 0), (0, INFO)), constant_values=-1))
    pick_x = ((code_x[0][None, :] == row_ids) | (code_x[1][None, :] == row_ids)).astype(BF16)
    pick_x, *x_pieces = lax.optimization_barrier((pick_x, *x_pieces))
    all_x = jnp.concatenate(x_pieces, axis=0)
    code, strength = from_zero(code), from_zero(strength)
    first, second = code[0][None, :] == row_ids, code[1][None, :] == row_ids
    scale = jnp.sum(
        jnp.where(first, strength[0][None, :], 0.0) + jnp.where(second, strength[1][None, :], 0.0),
        axis=1,
        keepdims=True,
    )
    pick = (first | second).astype(BF16)

    w_gate, w_up, w_down = gate_weight[0], up_weight[0], down_weight[0]

    def forward(x):
        gate, up = dot(x, w_gate, 1, 0), dot(x, w_up, 1, 0)
        sig = jax.nn.sigmoid(gate)
        return (gate * sig * up).astype(BF16), up * sig * (1.0 + gate * (1.0 - sig)), gate * sig

    def backward(g, for_gate, for_up):
        d_act = dot(g, w_down, 1, 1)
        return (d_act * for_gate).astype(BF16), (d_act * for_up).astype(BF16)

    x = exchange(dot(pick_x, all_x, 1, 0).astype(BF16))
    sent_g = (dot(pick, all_g, 1, 0) * scale).astype(BF16)
    x, sent_g = lax.optimization_barrier((x, sent_g))
    x_o = swapped(x)
    g = exchange(sent_g)
    forwards = forward(x), forward(x_o)
    forwards, g = lax.optimization_barrier((forwards, g))
    (act, for_gate, for_up), (act_o, for_gate_o, for_up_o) = forwards
    g_o = swapped(g)
    d_gate, d_up = backward(g, for_gate, for_up)
    own = dot(d_gate, w_gate, 1, 1) + dot(d_up, w_up, 1, 1)
    d_gate_o, d_up_o = backward(g_o, for_gate_o, for_up_o)
    for_other = (dot(d_gate_o, w_gate, 1, 1) + dot(d_up_o, w_up, 1, 1)).astype(BF16)
    from_other = swapped(for_other)
    contribution = (own + from_other.astype(F32)).astype(BF16)
    contribution, act, act_o, g, g_o = lax.optimization_barrier((contribution, act, act_o, g, g_o))
    back = exchange(contribution)

    slot_grad = dot(act, g, 0, 0) + dot(act_o, g_o, 0, 0)
    hidden = slot_grad.shape[0]
    down, across = hidden // 8, width // 128
    n_slots = slot_expert.shape[0]
    planes = n_slots // PLANE
    each = -(-down * across // n_slots)
    tiles = slot_grad.astype(BF16).reshape(down, 8, across, 128).transpose(0, 2, 1, 3)
    tiles = tiles.reshape(down * across, 8, 128)
    tiles = jnp.pad(tiles, ((0, each * n_slots - down * across), (0, 0), (0, 0)))
    tiles = tiles.reshape(planes, PLANE, each * 8, 128)

    def of_plane(v, d, dim):
        return lax.dynamic_index_in_dim(v, z_lo ^ d, dim, False)

    def along_z(piece, d):
        return lax.ppermute(piece, "zl", [(z, z ^ d) for z in range(planes)]) if d else piece

    sent = [of_plane(tiles, d, 0) for d in range(planes)]
    pieces = [along_z(piece, d) for d, piece in enumerate(sent)]
    parts = jnp.stack(pieces, axis=1)
    back, parts = lax.optimization_barrier((back, parts))
    parts = exchange(parts)
    partial = dot(pick, back, 0, 0).astype(BF16)
    token_grad = lax.psum_scatter(partial, ring, scatter_dimension=0, tiled=True)

    expert = slot_expert.reshape(planes, PLANE)
    expert = jnp.stack([of_plane(expert, d, 0) for d in range(planes)])
    sums = exchange(expert_sum(expert, parts))
    summed = jnp.stack([along_z(sums[:, d], d) for d in range(planes)])
    summed = jnp.concatenate([of_plane(summed, z, 0) for z in range(planes)])
    summed = summed.reshape(n_slots * each, 8, 128)[: down * across]
    down_grad = summed.reshape(down, across, 8, 128).transpose(0, 2, 1, 3).reshape(1, hidden, width)
    return token_grad, down_grad


def solution(mesh):
    fine = Mesh(mesh.devices.reshape(4, 4, 4, 2, 2), ("zl", "y", "x", "zh", "c"))
    ep, dp = ("zl", "y", "x"), ("zh", "c")
    token = P((*ep, *dp), None)
    return jax.shard_map(
        per_device,
        mesh=fine,
        in_specs=(token, token, token, token, P(), P(ep, None, dp), P(ep, None, dp), P(ep, dp, None)),
        out_specs=(token, P(ep, dp, None)),
        check_vma=False,
    )
```

```python
import jax
import jax.numpy as jnp
from jax import lax
from jax.experimental import pallas as pl
from jax.experimental.pallas import tpu as pltpu
from jax.sharding import Mesh, PartitionSpec as P

CAP = 5
INFO = 8
NZ = 8
PLANE = 16
EXPERTS = 32
F32 = jnp.float32
BF16 = jnp.bfloat16


def dot(a, b, ca, cb):
    return lax.dot_general(a, b, (((ca,), (cb,)), ((), ())), preferred_element_type=F32)


def expert_sum_kernel(expert_ref, parts_ref, out_ref, total):
    count, planes = parts_ref.shape[:2]
    total[...] = jnp.zeros_like(total)

    def add(j, carry):
        for d in range(planes):
            total[expert_ref[d, j]] += parts_ref[j, d].astype(F32)
        return carry

    def put(j, carry):
        for d in range(planes):
            out_ref[j, d] = total[expert_ref[d, j]].astype(BF16)
        return carry

    lax.fori_loop(0, count, add, 0)
    lax.fori_loop(0, count, put, 0)


def expert_sum(expert, parts):
    whole = pl.BlockSpec(memory_space=pltpu.VMEM)
    return pl.pallas_call(
        expert_sum_kernel,
        out_shape=jax.ShapeDtypeStruct(parts.shape, BF16),
        in_specs=[pl.BlockSpec(memory_space=pltpu.SMEM), whole],
        out_specs=whole,
        scratch_shapes=[pltpu.VMEM((EXPERTS, *parts.shape[2:]), F32)],
        compiler_params=pltpu.CompilerParams(vmem_limit_bytes=12 * 2**20),
    )(expert, parts)


def exchange(rows):
    chunks = rows.reshape(PLANE, rows.shape[0] // PLANE, *rows.shape[1:])
    got = lax.all_to_all(chunks, ("y", "x"), split_axis=0, concat_axis=0, tiled=True)
    return got.reshape(rows.shape)


def swapped(rows):
    return lax.ppermute(rows, "c", [(0, 1), (1, 0)])


def after(value, *earlier):
    return lax.optimization_barrier((value, *earlier))[0]


def ring_steps(own):
    def at(z):
        return (z % NZ) % 4 * 2 + (z % NZ) // 4

    up = [(at(z), at(z + 1)) for z in range(NZ)]
    down = [(at(z), at(z - 1)) for z in range(NZ)]
    below, above = [own], [own]
    for step in range(NZ // 2):
        below.append(lax.ppermute(below[-1], ("zl", "zh"), up))
        if step < NZ // 2 - 1:
            above.append(lax.ppermute(above[-1], ("zl", "zh"), down))
    return above + below[:0:-1], (below[3], above[3])


def per_device(
    tokens, cotangent, slot_choice, gate_values, slot_expert, gate_weight, up_weight, down_weight
):
    rows, width = tokens.shape
    items = 2 * rows
    z_lo, z_hi = lax.axis_index("zl"), lax.axis_index("zh")
    turn = z_hi * 4 + z_lo
    ring = ("zh", "zl")
    slot = slot_choice.T.reshape(items)
    weight = gate_values.T.reshape(items)
    order = jnp.arange(items, dtype=jnp.int32)
    earlier = (slot[:, None] == slot[None, :]) & (order[None, :] < order[:, None])
    place = jnp.sum(earlier.astype(jnp.int32), axis=1)
    high = lax.reduce_precision(weight, 8, 7)
    middle = lax.reduce_precision(weight - high, 8, 7)
    low = weight - high - middle
    facts = jnp.stack([slot.astype(F32), place.astype(F32), high, middle, low]).astype(BF16)
    facts = jnp.pad(facts, ((0, INFO - facts.shape[0]), (0, width - items)))

    x_pieces, started = ring_steps(jnp.concatenate([tokens, facts], axis=0))
    all_g = lax.all_gather(after(cotangent, *started), ring, axis=0, tiled=True)

    held = PLANE * NZ * CAP
    row_ids = jnp.arange(held, dtype=jnp.int32)[:, None]

    def flat(v):
        return jnp.moveaxis(v, 1, 0).reshape(2, -1)

    def chosen(pieces, away):
        info = jnp.stack([p[rows : rows + 5, :items] for p in pieces]).astype(F32).reshape(-1, 5, 2, rows)
        source = ((jnp.array(away, jnp.int32) + turn) % NZ)[:, None, None]
        code = info[:, 0].astype(jnp.int32) - z_lo * PLANE
        here = (code >= 0) & (code < PLANE)
        code = jnp.where(here, (code * NZ + source) * CAP + info[:, 1].astype(jnp.int32), -1)
        code_x = flat(jnp.pad(code, ((0, 0), (0, 0), (0, INFO)), constant_values=-1))
        pick_x = ((code_x[0][None, :] == row_ids) | (code_x[1][None, :] == row_ids)).astype(BF16)
        pick_x = lax.optimization_barrier(pick_x)
        return dot(pick_x, jnp.concatenate(pieces, axis=0), 1, 0), code, info[:, 2] + info[:, 3] + info[:, 4]

    near, code_n, strength_n = chosen(x_pieces[:4] + x_pieces[5:], [0, 1, 2, 3, 5, 6, 7])
    near = lax.optimization_barrier(near)
    far, code_f, strength_f = chosen(x_pieces[4:5], [4])
    code = jnp.concatenate([code_n[:4], code_f, code_n[4:]], axis=0)
    strength = jnp.concatenate([strength_n[:4], strength_f, strength_n[4:]], axis=0)

    def from_zero(v):
        return flat(lax.dynamic_slice_in_dim(jnp.concatenate([v, v], axis=0), NZ - turn, NZ, axis=0))

    code, strength = from_zero(code), from_zero(strength)
    first, second = code[0][None, :] == row_ids, code[1][None, :] == row_ids
    scale = jnp.sum(
        jnp.where(first, strength[0][None, :], 0.0) + jnp.where(second, strength[1][None, :], 0.0),
        axis=1,
        keepdims=True,
    )
    pick = (first | second).astype(BF16)

    w_gate, w_up, w_down = gate_weight[0], up_weight[0], down_weight[0]

    def forward(x):
        gate, up = dot(x, w_gate, 1, 0), dot(x, w_up, 1, 0)
        sig = jax.nn.sigmoid(gate)
        return (gate * sig * up).astype(BF16), up * sig * (1.0 + gate * (1.0 - sig)), gate * sig

    def backward(g, for_gate, for_up):
        d_act = dot(g, w_down, 1, 1)
        return (d_act * for_gate).astype(BF16), (d_act * for_up).astype(BF16)

    x = exchange((near + far).astype(BF16))
    sent_g = (dot(pick, all_g, 1, 0) * scale).astype(BF16)
    x, sent_g = lax.optimization_barrier((x, sent_g))
    x_o = swapped(x)
    g = exchange(sent_g)
    forwards = forward(x), forward(x_o)
    forwards, g = lax.optimization_barrier((forwards, g))
    (act, for_gate, for_up), (act_o, for_gate_o, for_up_o) = forwards
    g_o = swapped(g)
    d_gate, d_up = backward(g, for_gate, for_up)
    own = dot(d_gate, w_gate, 1, 1) + dot(d_up, w_up, 1, 1)
    d_gate_o, d_up_o = backward(g_o, for_gate_o, for_up_o)
    for_other = (dot(d_gate_o, w_gate, 1, 1) + dot(d_up_o, w_up, 1, 1)).astype(BF16)
    from_other = swapped(for_other)
    contribution = (own + from_other.astype(F32)).astype(BF16)
    contribution, act, act_o, g, g_o = lax.optimization_barrier((contribution, act, act_o, g, g_o))
    back = exchange(contribution)

    slot_grad = dot(act, g, 0, 0) + dot(act_o, g_o, 0, 0)
    hidden = slot_grad.shape[0]
    down, across = hidden // 8, width // 128
    n_slots = slot_expert.shape[0]
    planes = n_slots // PLANE
    each = -(-down * across // n_slots)
    tiles = slot_grad.astype(BF16).reshape(down, 8, across, 128).transpose(0, 2, 1, 3)
    tiles = tiles.reshape(down * across, 8, 128)
    tiles = jnp.pad(tiles, ((0, each * n_slots - down * across), (0, 0), (0, 0)))
    tiles = tiles.reshape(planes, PLANE, each * 8, 128)

    def of_plane(v, d, dim):
        return lax.dynamic_index_in_dim(v, z_lo ^ d, dim, False)

    def along_z(piece, d):
        return lax.ppermute(piece, "zl", [(z, z ^ d) for z in range(planes)]) if d else piece

    sent = [of_plane(tiles, d, 0) for d in range(planes)]
    pieces = [along_z(piece, d) for d, piece in enumerate(sent)]
    parts = jnp.stack(pieces, axis=1)
    back, parts = lax.optimization_barrier((back, parts))
    parts = exchange(parts)
    partial = dot(pick, back, 0, 0).astype(BF16)
    token_grad = lax.psum_scatter(partial, ring, scatter_dimension=0, tiled=True)

    expert = slot_expert.reshape(planes, PLANE)
    expert = jnp.stack([of_plane(expert, d, 0) for d in range(planes)])
    sums = exchange(expert_sum(expert, parts))
    summed = jnp.stack([along_z(sums[:, d], d) for d in range(planes)])
    summed = jnp.concatenate([of_plane(summed, z, 0) for z in range(planes)])
    summed = summed.reshape(n_slots * each, 8, 128)[: down * across]
    down_grad = summed.reshape(down, across, 8, 128).transpose(0, 2, 1, 3).reshape(1, hidden, width)
    return token_grad, down_grad


def solution(mesh):
    fine = Mesh(mesh.devices.reshape(4, 4, 4, 2, 2), ("zl", "y", "x", "zh", "c"))
    ep, dp = ("zl", "y", "x"), ("zh", "c")
    token = P((*ep, *dp), None)
    return jax.shard_map(
        per_device,
        mesh=fine,
        in_specs=(token, token, token, token, P(), P(ep, None, dp), P(ep, None, dp), P(ep, dp, None)),
        out_specs=(token, P(ep, dp, None)),
        check_vma=False,
    )
```
